32 devices in a mesh: chan: 8 (over y, x, core), win: 4 (over z).
Axes of the slice: x: 2, y: 2, z: 4, core: 2. Of those that a mesh axis runs over, the one named last changes fastest.
Arguments:
- spectra: bfloat16 [16, 256, 4096], P('win', 'chan'), may hold values from -80 to 80
- quality: int32 [256], P('chan'), may hold values 0 or 1
- source_block: int32 [2], replicated, may hold values from 0 to 31
Outputs:
- correlations: bfloat16 [2, 256, 8, 512], P(None, ('chan', 'win'))
The draws below stay inside these ranges and needn't reach their ends.
All inputs are finite; a program needn't handle non-finite values. No bound on the sum of `quality` on one device may be relied on, other than what follows from the above.
Results may differ from the reference program's by a relative error of at most 0.0045.
Values may be sent and summed in bfloat16 or wider, within the bound.
No kernel may reach another device: no remote copies, remote signals or barrier semaphores. Data moves between devices by JAX's collectives and lax.ppermute only.
A program may use at most 192 MiB of HBM per device.

```python
import math
import jax
import jax.numpy as jnp
from jax import lax

F = 2048
L = 512
SRC = 8
STEPS = 2
CHANNELS = 256
WINDOWS = 16


def draw_spectra(key, part):
    first = jax.random.fold_in(key, 0)
    second = jax.random.fold_in(key, 1)
    fourth = jax.random.fold_in(key, 3)
    shape = (WINDOWS, CHANNELS, 2 * F)
    base = jnp.clip(jax.random.normal(first, shape, jnp.float32), -6.0, 6.0)
    scales = jnp.exp(jax.random.uniform(second, (WINDOWS, CHANNELS, 1), jnp.float32, 0.0, math.log(10.0)))
    shaping = jnp.exp(jax.random.uniform(fourth, (1, 1, 2 * F), jnp.float32, -0.5, 0.5))
    return (base * scales * shaping).astype(jnp.bfloat16)


def plant(result, own_key, least, largest):
    index_at = [jax.random.randint(jax.random.fold_in(own_key, axis), (), 0, length) for axis, length in enumerate(result.shape)]
    widest = result.shape.index(max(result.shape))
    beside = index_at[:widest] + [(index_at[widest] + 1) % result.shape[widest]] + index_at[widest + 1:]
    return result.at[tuple(index_at)].set(least).at[tuple(beside)].set(largest)


def setup_inputs(seed: int = 0) -> dict:
    key_of = jax.random.split(jax.random.key(seed), 4)
    return {
        "spectra": draw_spectra(jax.random.fold_in(key_of[3], 71), 0),
        "quality": plant((jax.random.randint(key_of[1], (CHANNELS,), 0, 8) < 7).astype(jnp.int32), jax.random.fold_in(key_of[1], 1), 0, 1),
        "source_block": jax.random.randint(key_of[2], (STEPS,), 0, CHANNELS // SRC).astype(jnp.int32),
    }


def lag_table(bins, lags, factor):
    bin_index = lax.iota(jnp.int32, bins)[:, None]
    shifts = lax.iota(jnp.int32, lags)[None, :] - lags // 2
    residue = jnp.mod(bin_index * shifts, 2 * bins)
    phase_angle = residue.astype(jnp.float32) * (2.0 * math.pi / (2 * bins))
    return jnp.concatenate([jnp.cos(phase_angle), -jnp.sin(phase_angle)], axis=0) * factor

def whiten(block, quality):
    values = block.astype(jnp.float32)
    bins = values.shape[-1] // 2
    energy = lax.optimization_barrier(jnp.sum(values * values, axis=-1)) / bins
    weights = quality.astype(jnp.float32)[None, :] / jnp.sqrt(energy + 1e-06)
    return (values * weights[:, :, None]).astype(jnp.bfloat16)

def cross_spectra(sources, receivers):
    bins = sources.shape[-1] // 2
    src_real = sources[:, :, :bins].astype(jnp.float32)
    src_imag = sources[:, :, bins:].astype(jnp.float32)
    rec_real = receivers[:, :, :bins].astype(jnp.float32)
    rec_imag = receivers[:, :, bins:].astype(jnp.float32)
    real_part = jnp.einsum('wsf,wrf->rsf', src_real, rec_real) + jnp.einsum('wsf,wrf->rsf', src_imag, rec_imag)
    imag_part = jnp.einsum('wsf,wrf->rsf', src_real, rec_imag) - jnp.einsum('wsf,wrf->rsf', src_imag, rec_real)
    return jnp.concatenate([real_part, imag_part], axis=-1)

def reference(spectra, quality, source_block):
    window_count, channel_count, row_width = spectra.shape
    bins = row_width // 2
    transform = lag_table(bins, L, 1.0 / math.sqrt(row_width * window_count))

    def one_window(carry, index):
        block = lax.dynamic_slice_in_dim(spectra, index, 1, 0)
        whitened = whiten(block, quality)
        terms = []
        for step in range(STEPS):
            start = (source_block[step] * SRC).astype(jnp.int32)
            sources = lax.dynamic_slice_in_dim(whitened, start, SRC, 1)
            terms.append(cross_spectra(sources, whitened))
        return (carry + jnp.stack(terms), None)
    empty = jnp.zeros((STEPS, channel_count, SRC, row_width), jnp.float32)
    cross, _ = lax.scan(one_window, empty, jnp.arange(window_count, dtype=jnp.int32))
    lagged = jnp.dot(cross.reshape(-1, row_width), transform, precision=lax.Precision.HIGHEST, preferred_element_type=jnp.float32)
    return lagged.reshape(STEPS, channel_count, SRC, L).astype(jnp.bfloat16)
```

```python
import functools
import math

import jax
import jax.numpy as jnp
from jax import lax
from jax.experimental import pallas as pl
from jax.experimental.pallas import tpu as pltpu
from jax.sharding import PartitionSpec as P

L = 512
SRC = 8
STEPS = 2
LANES = 128
BINS_PER_CHUNK = 256
TABLE_ROWS = 64
EPS = 1e-06
F32 = jnp.float32
BF16 = jnp.bfloat16
VMEM_LIMIT = 48 * 1024 * 1024


def smem():
    return pl.BlockSpec(memory_space=pltpu.SMEM)


def vmem():
    return pl.BlockSpec(memory_space=pltpu.VMEM)


def params():
    return pltpu.CompilerParams(vmem_limit_bytes=VMEM_LIMIT)


def column(count, read):
    rows = lax.broadcasted_iota(jnp.int32, (count, 1), 0)
    result = jnp.zeros((count, 1), F32)
    for row in range(count):
        result = jnp.where(rows == row, read(row), result)
    return result


def whitened_rows(values, quality):
    energy = jnp.sum(values * values, axis=-1, keepdims=True) / (values.shape[-1] // 2)
    return (values * (quality / jnp.sqrt(energy + EPS))).astype(BF16)


def sources_kernel(scalars, quality, spectra, mine, other):
    for place, out in enumerate((mine, other)):
        held, base = scalars[1 + 2 * place], scalars[2 + 2 * place]
        aligned = pl.multiple_of(base // 16 * 16, 16)
        upper = base % 16 != 0
        flags = column(SRC, lambda row: (quality[base + row] * held).astype(F32))
        for window in range(spectra.shape[0]):
            rows = spectra[window, pl.ds(aligned, 16), :].astype(F32)
            values = jnp.where(upper, rows[SRC:], rows[:SRC])
            out[window] = whitened_rows(values, flags)


def receivers_kernel(quality, spectra, out):
    owners, windows, rows, _ = out.shape
    flags = column(owners * rows, lambda row: quality[row].astype(F32))
    for window in range(windows):
        values = whitened_rows(spectra[window].astype(F32), flags).astype(F32)
        for owner in range(owners):
            out[owner, window] = values[owner * rows : (owner + 1) * rows]


def table_kernel(factor, out, turn_cos, turn_sin, base_cos, base_sin):
    bins, lags = out.shape[0] // 2, out.shape[1]

    def angles(count, stride):
        rows = lax.broadcasted_iota(jnp.int32, (count, lags), 0) * stride
        shifts = lax.broadcasted_iota(jnp.int32, (count, lags), 1) - lags // 2
        residue = (rows * shifts) & (2 * bins - 1)
        residue = jnp.where(residue >= bins, residue - 2 * bins, residue)
        return residue.astype(F32) * (2.0 * math.pi / (2 * bins))

    turns = angles(bins // TABLE_ROWS, TABLE_ROWS)
    turn_cos[...] = jnp.cos(turns) * factor
    turn_sin[...] = jnp.sin(turns) * factor
    base = angles(TABLE_ROWS, 1)
    base_cos[...] = jnp.cos(base)
    base_sin[...] = jnp.sin(base)

    @pl.loop(0, bins // TABLE_ROWS)
    def _(turn):
        far_cos, far_sin = turn_cos[pl.ds(turn, 1), :], turn_sin[pl.ds(turn, 1), :]
        near_cos, near_sin = base_cos[...], base_sin[...]
        start = pl.multiple_of(turn * TABLE_ROWS, TABLE_ROWS)
        out[pl.ds(start, TABLE_ROWS), :] = (near_cos * far_cos - near_sin * far_sin).astype(BF16)
        out[pl.ds(bins + start, TABLE_ROWS), :] = (
            -(near_sin * far_cos + near_cos * far_sin)
        ).astype(BF16)


def lagged_kernel(owners, mine, other, receivers, table, *rest):
    outs, (even, odd, total) = rest[:-3], rest[-3:]
    _, windows, rows, width = receivers.shape
    bins = width // 2
    chunk = BINS_PER_CHUNK
    chunks = bins // chunk

    def cross(index, held):
        for tile in range(chunk // LANES):
            at = index * chunk + tile * LANES
            if not isinstance(index, int):
                at = pl.multiple_of(at, LANES)
            real, imag = pl.ds(at, LANES), pl.ds(bins + at, LANES)
            sources = [
                [(ref[w, :, real].astype(F32), ref[w, :, imag].astype(F32)) for w in range(windows)]
                for ref in (mine, other)
            ]
            for place in range(len(outs)):
                owner = owners[place]
                for row in range(rows):
                    sums = [[None, None], [None, None]]
                    for w in range(windows):
                        rec_real = receivers[owner, w, pl.ds(row, 1), real]
                        rec_imag = receivers[owner, w, pl.ds(row, 1), imag]
                        for s in range(2):
                            src_real, src_imag = sources[s][w]
                            re = src_real * rec_real + src_imag * rec_imag
                            im = src_real * rec_imag - src_imag * rec_real
                            sums[s][0] = re if w == 0 else sums[s][0] + re
                            sums[s][1] = im if w == 0 else sums[s][1] + im
                    start = (place * rows + row) * 2 * SRC
                    for part in range(2):
                        both = jnp.concatenate([sums[0][part], sums[1][part]], axis=0)
                        lane = part * chunk + tile * LANES
                        held[start : start + 2 * SRC, lane : lane + LANES] = both.astype(BF16)

    def lags(index, held, first=False):
        at = index * chunk
        if not isinstance(index, int):
            at = pl.multiple_of(at, chunk)
        product = jnp.dot(
            held[:, :chunk], table[pl.ds(at, chunk), :], preferred_element_type=F32
        ) + jnp.dot(
            held[:, chunk:], table[pl.ds(bins + at, chunk), :], preferred_element_type=F32
        )
        total[...] = product if first else total[...] + product

    cross(0, even)
    cross(1, odd)
    lags(0, even, first=True)

    @pl.loop(0, chunks // 2 - 1)
    def _(pair):
        cross(2 * pair + 2, even)
        lags(2 * pair + 1, odd)
        cross(2 * pair + 3, odd)
        lags(2 * pair + 2, even)

    lags(chunks - 1, odd)
    for place, out in enumerate(outs):
        for row in range(rows):
            start = (place * rows + row) * 2 * SRC
            out[row] = total[start : start + 2 * SRC, :].astype(out.dtype)


def stack_kernel(scalars, own, *rest):
    received, out = rest[:-1], rest[-1]
    step = scalars[0]
    for row in range(own.shape[0]):
        total = own[row]
        for ref in received:
            total = total + ref[row].astype(F32)
        out[step, row] = total[:SRC].astype(BF16)
        out[1 - step, row] = total[SRC:].astype(BF16)


def lagged_call(owners, mine, other, receivers, table, dtype):
    count = owners.shape[0]
    _, windows, rows, width = receivers.shape
    lines = count * rows * 2 * SRC
    shape = jax.ShapeDtypeStruct((rows, 2 * SRC, L), dtype)
    return pl.pallas_call(
        lagged_kernel,
        out_shape=[shape] * count,
        in_specs=[smem(), vmem(), vmem(), vmem(), vmem()],
        out_specs=[vmem()] * count,
        scratch_shapes=[
            pltpu.VMEM((lines, 2 * BINS_PER_CHUNK), BF16),
            pltpu.VMEM((lines, 2 * BINS_PER_CHUNK), BF16),
            pltpu.VMEM((lines, L), F32),
        ],
        compiler_params=params(),
        cost_estimate=pl.CostEstimate(
            flops=2 * lines * width * L, bytes_accessed=2 * width * L, transcendentals=0
        ),
    )(owners, mine, other, receivers, table)


def exchange(value, axis, distance):
    size = lax.axis_size(axis)
    return lax.ppermute(value, axis, [(i, i ^ distance) for i in range(size)])


def body(spectra, quality, source_block):
    windows, channels, width = spectra.shape
    group, groups = lax.axis_index("chan"), lax.axis_size("chan")
    place, places = lax.axis_index("win"), lax.axis_size("win")
    bins = width // 2
    rows = channels // places
    factor = 1.0 / math.sqrt(width * windows * places)

    core = group % 2
    blocks = jnp.stack([source_block[core], source_block[1 - core]]).astype(jnp.int32)
    per_group = channels // SRC
    held = (blocks // per_group == group).astype(jnp.int32)
    base = blocks % per_group * SRC
    scalars = jnp.stack([core, held[0], base[0], held[1], base[1]]).astype(jnp.int32)

    candidate = jax.ShapeDtypeStruct((windows, SRC, width), BF16)
    mine, other = pl.pallas_call(
        sources_kernel,
        out_shape=[candidate, candidate],
        in_specs=[smem(), smem(), vmem()],
        out_specs=[vmem(), vmem()],
        compiler_params=params(),
    )(scalars, quality, spectra)

    receivers = pl.pallas_call(
        receivers_kernel,
        out_shape=jax.ShapeDtypeStruct((places, windows, rows, width), F32),
        in_specs=[smem(), vmem()],
        out_specs=vmem(),
        compiler_params=params(),
    )(quality, spectra)
    table = pl.pallas_call(
        functools.partial(table_kernel, factor),
        out_shape=jax.ShapeDtypeStruct((width, L), BF16),
        out_specs=vmem(),
        scratch_shapes=[pltpu.VMEM((bins // TABLE_ROWS, L), F32)] * 2
        + [pltpu.VMEM((TABLE_ROWS, L), F32)] * 2,
        compiler_params=params(),
    )()

    both = mine + exchange(other, "chan", 1)
    halves = [both[: windows // 2], both[windows // 2 :]]
    distances = [1 << bit for bit in range(1, (groups - 1).bit_length())]
    for one, two in zip(distances, reversed(distances), strict=True):
        halves = [halves[0] + exchange(halves[0], "chan", one), halves[1] + exchange(halves[1], "chan", two)]
    mine = jnp.concatenate(halves)
    other = exchange(mine, "chan", 1)

    far_first = sorted(range(1, places), key=lambda d: (-(d.bit_length()), d))
    received = []
    for distance in far_first:
        owners = jnp.reshape(place ^ distance, (1,)).astype(jnp.int32)
        (partial,) = lagged_call(owners, mine, other, receivers, table, BF16)
        received.append(exchange(partial, "win", distance))
    owners = jnp.reshape(place, (1,)).astype(jnp.int32)
    (own,) = lagged_call(owners, mine, other, receivers, table, F32)

    return pl.pallas_call(
        stack_kernel,
        out_shape=jax.ShapeDtypeStruct((STEPS, rows, SRC, L), BF16),
        in_specs=[smem(), vmem()] + [vmem()] * len(received),
        out_specs=vmem(),
        compiler_params=params(),
    )(scalars, own, *received)


def solution(mesh):
    return jax.shard_map(
        body,
        mesh=mesh,
        in_specs=(P("win", "chan", None), P("chan"), P()),
        out_specs=P(None, ("chan", "win"), None, None),
        check_vma=False,
    )
```

```python
import functools
import math

import jax
import jax.numpy as jnp
from jax import lax
from jax.experimental import pallas as pl
from jax.experimental.pallas import tpu as pltpu
from jax.sharding import PartitionSpec as P

L = 512
SRC = 8
STEPS = 2
LANES = 128
BINS_PER_CHUNK = 256
TABLE_ROWS = 64
EPS = 1e-06
F32 = jnp.float32
BF16 = jnp.bfloat16
VMEM_LIMIT = 16 * 1024 * 1024


def smem():
    return pl.BlockSpec(memory_space=pltpu.SMEM)


def vmem():
    return pl.BlockSpec(memory_space=pltpu.VMEM)


def params():
    return pltpu.CompilerParams(vmem_limit_bytes=VMEM_LIMIT)


def column(count, read):
    rows = lax.broadcasted_iota(jnp.int32, (count, 1), 0)
    result = jnp.zeros((count, 1), F32)
    for row in range(count):
        result = jnp.where(rows == row, read(row), result)
    return result


def whitened_rows(values, quality):
    energy = jnp.sum(values * values, axis=-1, keepdims=True) / (values.shape[-1] // 2)
    return (values * (quality / jnp.sqrt(energy + EPS))).astype(BF16)


def sources_kernel(blocks, quality, spectra, mine, other):
    group = lax.axis_index("chan")
    per_group = spectra.shape[1] // SRC
    for place, out in enumerate((mine, other)):
        block = blocks[(group + place) % 2]
        held = (block // per_group == group).astype(jnp.int32)
        base = block % per_group * SRC
        aligned = pl.multiple_of(base // 16 * 16, 16)
        upper = base % 16 != 0
        flags = column(SRC, lambda row: (quality[base + row] * held).astype(F32))
        for window in range(spectra.shape[0]):
            rows = spectra[window, pl.ds(aligned, 16), :].astype(F32)
            values = jnp.where(upper, rows[SRC:], rows[:SRC])
            out[window] = whitened_rows(values, flags)


def receivers_kernel(quality, spectra, out):
    owners, windows, rows, _ = out.shape
    flags = column(owners * rows, lambda row: quality[row].astype(F32))
    for window in range(windows):
        values = whitened_rows(spectra[window].astype(F32), flags).astype(F32)
        for owner in range(owners):
            out[owner, window] = values[owner * rows : (owner + 1) * rows]


def table_kernel(factor, out, turn_cos, turn_sin, base_cos, base_sin):
    bins, lags = out.shape[0] // 2, out.shape[1]

    def angles(count, stride):
        rows = lax.broadcasted_iota(jnp.int32, (count, lags), 0) * stride
        shifts = lax.broadcasted_iota(jnp.int32, (count, lags), 1) - lags // 2
        residue = (rows * shifts) & (2 * bins - 1)
        residue = jnp.where(residue >= bins, residue - 2 * bins, residue)
        return residue.astype(F32) * (2.0 * math.pi / (2 * bins))

    turns = angles(bins // TABLE_ROWS, TABLE_ROWS)
    turn_cos[...] = jnp.cos(turns) * factor
    turn_sin[...] = jnp.sin(turns) * factor
    base = angles(TABLE_ROWS, 1)
    base_cos[...] = jnp.cos(base)
    base_sin[...] = jnp.sin(base)

    @pl.loop(0, bins // TABLE_ROWS)
    def _(turn):
        far_cos, far_sin = turn_cos[pl.ds(turn, 1), :], turn_sin[pl.ds(turn, 1), :]
        near_cos, near_sin = base_cos[...], base_sin[...]
        start = pl.multiple_of(turn * TABLE_ROWS, TABLE_ROWS)
        out[pl.ds(start, TABLE_ROWS), :] = (near_cos * far_cos - near_sin * far_sin).astype(BF16)
        out[pl.ds(bins + start, TABLE_ROWS), :] = (
            -(near_sin * far_cos + near_cos * far_sin)
        ).astype(BF16)


def lagged_kernel(distances, mine, other, receivers, table, *rest):
    owners = [lax.axis_index("win") ^ distance for distance in distances]
    outs, (even, odd, total) = rest[:-3], rest[-3:]
    _, windows, rows, width = receivers.shape
    bins = width // 2
    chunk = BINS_PER_CHUNK
    chunks = bins // chunk

    def cross(index, held):
        for tile in range(chunk // LANES):
            at = index * chunk + tile * LANES
            if not isinstance(index, int):
                at = pl.multiple_of(at, LANES)
            real, imag = pl.ds(at, LANES), pl.ds(bins + at, LANES)
            sources = [
                [(ref[w, :, real].astype(F32), ref[w, :, imag].astype(F32)) for w in range(windows)]
                for ref in (mine, other)
            ]
            for place in range(len(outs)):
                owner = owners[place]
                for row in range(rows):
                    sums = [[None, None], [None, None]]
                    for w in range(windows):
                        rec_real = receivers[owner, w, pl.ds(row, 1), real]
                        rec_imag = receivers[owner, w, pl.ds(row, 1), imag]
                        for s in range(2):
                            src_real, src_imag = sources[s][w]
                            re = src_real * rec_real + src_imag * rec_imag
                            im = src_real * rec_imag - src_imag * rec_real
                            sums[s][0] = re if w == 0 else sums[s][0] + re
                            sums[s][1] = im if w == 0 else sums[s][1] + im
                    start = (place * rows + row) * 2 * SRC
                    for part in range(2):
                        both = jnp.concatenate([sums[0][part], sums[1][part]], axis=0)
                        lane = part * chunk + tile * LANES
                        held[start : start + 2 * SRC, lane : lane + LANES] = both.astype(BF16)

    def lags(index, held, first=False):
        at = index * chunk
        if not isinstance(index, int):
            at = pl.multiple_of(at, chunk)
        product = jnp.dot(
            held[:, :chunk], table[pl.ds(at, chunk), :], preferred_element_type=F32
        ) + jnp.dot(
            held[:, chunk:], table[pl.ds(bins + at, chunk), :], preferred_element_type=F32
        )
        total[...] = product if first else total[...] + product

    cross(0, even)
    cross(1, odd)
    lags(0, even, first=True)

    @pl.loop(0, chunks // 2 - 1)
    def _(pair):
        cross(2 * pair + 2, even)
        lags(2 * pair + 1, odd)
        cross(2 * pair + 3, odd)
        lags(2 * pair + 2, even)

    lags(chunks - 1, odd)
    for place, out in enumerate(outs):
        for row in range(rows):
            start = (place * rows + row) * 2 * SRC
            out[row] = total[start : start + 2 * SRC, :].astype(out.dtype)


def stack_kernel(own, *rest):
    received, out = rest[:-1], rest[-1]
    step = lax.axis_index("chan") % 2
    for row in range(own.shape[0]):
        total = own[row]
        for ref in received:
            total = total + ref[row].astype(F32)
        out[step, row] = total[:SRC].astype(BF16)
        out[1 - step, row] = total[SRC:].astype(BF16)


def lagged_call(distances, mine, other, receivers, table, dtype):
    count = len(distances)
    _, windows, rows, width = receivers.shape
    lines = count * rows * 2 * SRC
    shape = jax.ShapeDtypeStruct((rows, 2 * SRC, L), dtype)
    return pl.pallas_call(
        functools.partial(lagged_kernel, distances),
        out_shape=[shape] * count,
        in_specs=[vmem()] * 4,
        out_specs=[vmem()] * count,
        scratch_shapes=[
            pltpu.VMEM((lines, 2 * BINS_PER_CHUNK), BF16),
            pltpu.VMEM((lines, 2 * BINS_PER_CHUNK), BF16),
            pltpu.VMEM((lines, L), F32),
        ],
        compiler_params=params(),
        cost_estimate=pl.CostEstimate(
            flops=2 * lines * width * L, bytes_accessed=2 * width * L, transcendentals=0
        ),
    )(mine, other, receivers, table)


def exchange(value, axis, distance):
    size = lax.axis_size(axis)
    return lax.ppermute(value, axis, [(i, i ^ distance) for i in range(size)])


def body(spectra, quality, source_block):
    windows, channels, width = spectra.shape
    groups, places = lax.axis_size("chan"), lax.axis_size("win")
    bins = width // 2
    rows = channels // places
    factor = 1.0 / math.sqrt(width * windows * places)

    candidate = jax.ShapeDtypeStruct((windows, SRC, width), BF16)
    mine, other = pl.pallas_call(
        sources_kernel,
        out_shape=[candidate, candidate],
        in_specs=[smem(), smem(), vmem()],
        out_specs=[vmem(), vmem()],
        compiler_params=params(),
    )(source_block, quality, spectra)

    both = mine + exchange(other, "chan", 1)
    both, spectra = lax.optimization_barrier((both, spectra))
    halves = [both[: windows // 2], both[windows // 2 :]]
    receivers = pl.pallas_call(
        receivers_kernel,
        out_shape=jax.ShapeDtypeStruct((places, windows, rows, width), F32),
        in_specs=[smem(), vmem()],
        out_specs=vmem(),
        compiler_params=params(),
    )(quality, spectra)
    table = pl.pallas_call(
        functools.partial(table_kernel, factor),
        out_shape=jax.ShapeDtypeStruct((width, L), BF16),
        out_specs=vmem(),
        scratch_shapes=[pltpu.VMEM((bins // TABLE_ROWS, L), F32)] * 2
        + [pltpu.VMEM((TABLE_ROWS, L), F32)] * 2,
        compiler_params=params(),
    )()

    distances = [1 << bit for bit in range(1, (groups - 1).bit_length())]
    for index, (one, two) in enumerate(zip(distances, reversed(distances), strict=True)):
        if index == 1:
            halves, receivers, table = lax.optimization_barrier((halves, receivers, table))
        halves = [halves[0] + exchange(halves[0], "chan", one), halves[1] + exchange(halves[1], "chan", two)]
    mine = jnp.concatenate(halves)
    other = exchange(mine, "chan", 1)

    far_first = sorted(range(1, places), key=lambda d: (-(d.bit_length()), d))
    received = []
    for distance in far_first:
        (partial,) = lagged_call([distance], mine, other, receivers, table, BF16)
        received.append(exchange(partial, "win", distance))
    (own,) = lagged_call([0], mine, other, receivers, table, F32)

    return pl.pallas_call(
        stack_kernel,
        out_shape=jax.ShapeDtypeStruct((STEPS, rows, SRC, L), BF16),
        in_specs=[vmem()] * (1 + len(received)),
        out_specs=vmem(),
        compiler_params=params(),
    )(own, *received)


def solution(mesh):
    return jax.shard_map(
        body,
        mesh=mesh,
        in_specs=(P("win", "chan", None), P("chan"), P()),
        out_specs=P(None, ("chan", "win"), None, None),
        check_vma=False,
    )
```

```python
import functools
import math

import jax
import jax.numpy as jnp
from jax import lax
from jax.experimental import pallas as pl
from jax.experimental.pallas import tpu as pltpu
from jax.sharding import PartitionSpec as P

L = 512
SRC = 8
STEPS = 2
LANES = 128
TILES_PER_DOT = 4
TABLE_ROWS = 64
EPS = 1e-06
F32 = jnp.float32
BF16 = jnp.bfloat16
VMEM_LIMIT = 16 * 1024 * 1024


def smem():
    return pl.BlockSpec(memory_space=pltpu.SMEM)


def vmem():
    return pl.BlockSpec(memory_space=pltpu.VMEM)


def params():
    return pltpu.CompilerParams(vmem_limit_bytes=VMEM_LIMIT)


def column(count, read):
    rows = lax.broadcasted_iota(jnp.int32, (count, 1), 0)
    result = jnp.zeros((count, 1), F32)
    for row in range(count):
        result = jnp.where(rows == row, read(row), result)
    return result


def whitened_rows(values, quality):
    energy = jnp.sum(values * values, axis=-1, keepdims=True) / (values.shape[-1] // 2)
    return (values * (quality / jnp.sqrt(energy + EPS))).astype(BF16).astype(F32)


def sources_kernel(blocks_in, quality_in, spectra_in, *rest):
    outs, (blocks, quality, spectra, sems) = rest[:-4], rest[-4:]
    windows, channels, width = spectra.shape
    bins, part = width // 2, width // 4
    copies = [
        pltpu.make_async_copy(blocks_in, blocks, sems.at[windows]),
        pltpu.make_async_copy(quality_in, quality, sems.at[windows + 1]),
    ] + [
        pltpu.make_async_copy(spectra_in.at[window], spectra.at[window], sems.at[window])
        for window in range(windows)
    ]
    for copy in copies:
        copy.start()
    copies[0].wait()
    copies[1].wait()
    group = lax.axis_index("chan")
    even = group % 2 == 0
    per_group = channels // SRC
    chosen = []
    for step in range(STEPS):
        block = blocks[step]
        held = (block // per_group == group).astype(jnp.int32)
        base = block % per_group * SRC
        flags = column(SRC, lambda row: (quality[base + row] * held).astype(F32))
        chosen.append((pl.multiple_of(base // 16 * 16, 16), base % 16 != 0, flags))
    for window in range(windows):
        copies[2 + window].wait()
        for step, (aligned, upper, flags) in enumerate(chosen):
            rows = spectra[window, pl.ds(aligned, 16), :].astype(F32)
            values = whitened_rows(jnp.where(upper, rows[SRC:], rows[:SRC]), flags)
            low = jnp.concatenate([values[:, :part], values[:, bins : bins + part]], axis=1)
            high = jnp.concatenate([values[:, part:bins], values[:, bins + part :]], axis=1)
            outs[step][window] = jnp.where(even, low, high).astype(BF16)
            outs[STEPS + step][window] = jnp.where(even, high, low).astype(BF16)


def receivers_kernel(quality, spectra, out):
    owners, windows, rows, _ = out.shape
    flags = column(owners * rows, lambda row: quality[row].astype(F32))
    for window in range(windows):
        values = whitened_rows(spectra[window].astype(F32), flags)
        for owner in range(owners):
            out[owner, window] = values[owner * rows : (owner + 1) * rows]


def table_kernel(factor, out, turn_cos, turn_sin, base_cos, base_sin):
    bins, lags = out.shape[0] // 2, out.shape[1]

    def angles(count, stride):
        rows = lax.broadcasted_iota(jnp.int32, (count, lags), 0) * stride
        shifts = lax.broadcasted_iota(jnp.int32, (count, lags), 1) - lags // 2
        residue = (rows * shifts) & (2 * bins - 1)
        residue = jnp.where(residue >= bins, residue - 2 * bins, residue)
        return residue.astype(F32) * (2.0 * math.pi / (2 * bins))

    turns = angles(bins // TABLE_ROWS, TABLE_ROWS)
    turn_cos[...] = jnp.cos(turns) * factor
    turn_sin[...] = jnp.sin(turns) * factor
    base = angles(TABLE_ROWS, 1)
    base_cos[...] = jnp.cos(base)
    base_sin[...] = jnp.sin(base)

    @pl.loop(0, bins // TABLE_ROWS)
    def _(turn):
        far_cos, far_sin = turn_cos[pl.ds(turn, 1), :], turn_sin[pl.ds(turn, 1), :]
        near_cos, near_sin = base_cos[...], base_sin[...]
        start = pl.multiple_of(turn * TABLE_ROWS, TABLE_ROWS)
        out[pl.ds(start, TABLE_ROWS), :] = (near_cos * far_cos - near_sin * far_sin).astype(BF16)
        out[pl.ds(bins + start, TABLE_ROWS), :] = (
            -(near_sin * far_cos + near_cos * far_sin)
        ).astype(BF16)


def lagged_kernel(distances, plan, carried, zeros, *refs):
    steps = sorted({step for _, present in plan for step in present})
    count = sum(len(present) for _, present in plan)
    sources, (receivers, table), refs = list(refs[:count]), refs[count : count + 2], refs[count + 2 :]
    carry = refs[: len(carried)]
    if zeros:
        refs, out = refs[:-1], refs[-1]
        out[...] = jnp.zeros_like(out)
    outs = refs[len(refs) - len(steps) :]
    core = lax.axis_index("chan") % 2
    _, windows, rows, width = receivers.shape
    bins, part = width // 2, width // 4
    lines = rows * SRC
    depth = TILES_PER_DOT * LANES

    def cross_tile(pair, start, at):
        real, imag = pl.ds(at, LANES), pl.ds(part + at, LANES)
        src = [
            [(ref[w, :, real].astype(F32), ref[w, :, imag].astype(F32)) for w in range(windows)]
            for ref in pair
        ]
        real = pl.ds(pl.multiple_of(start + at, LANES), LANES)
        imag = pl.ds(pl.multiple_of(bins + start + at, LANES), LANES)
        found = [[[], []] for _ in pair]
        for distance in distances:
            owner = lax.axis_index("win") ^ distance
            for row in range(rows):
                sums = [[None, None] for _ in pair]
                for w in range(windows):
                    rec_real = receivers[owner, w, pl.ds(row, 1), real]
                    rec_imag = receivers[owner, w, pl.ds(row, 1), imag]
                    for s in range(len(pair)):
                        src_real, src_imag = src[s][w]
                        re = src_real * rec_real + src_imag * rec_imag
                        im = src_real * rec_imag - src_imag * rec_real
                        sums[s][0] = re if w == 0 else sums[s][0] + re
                        sums[s][1] = im if w == 0 else sums[s][1] + im
                for s in range(len(pair)):
                    for p in range(2):
                        found[s][p].append(sums[s][p])
        return [
            jnp.concatenate(
                [
                    jnp.concatenate(one[p][row : row + 2], axis=0).astype(BF16)
                    for one in found
                    for row in range(0, len(one[p]), 2)
                ],
                axis=0,
            )
            for p in range(2)
        ]

    totals = {}
    for ref, step in zip(carry, carried, strict=True):
        held = [ref[distance * rows // 2 + pair] for distance in distances for pair in range(rows // 2)]
        totals[step] = jnp.concatenate(held, axis=0)
    for other, present in plan:
        pair, sources = sources[: len(present)], sources[len(present) :]
        start = (1 - core if other else core) * part
        for chunk in range(part // depth):
            at = chunk * depth
            tiles = [cross_tile(pair, start, at + tile * LANES) for tile in range(TILES_PER_DOT)]
            for p in range(2):
                cross = jnp.concatenate([tile[p] for tile in tiles], axis=1)
                where = pl.ds(pl.multiple_of(p * bins + start + at, depth), depth)
                product = jnp.dot(cross, table[where, :], preferred_element_type=F32)
                for place, step in enumerate(present):
                    height = lines * len(distances)
                    piece = product[place * height : (place + 1) * height]
                    totals[step] = totals[step] + piece if step in totals else piece
    for out, step in zip(outs, steps, strict=True):
        for pair in range(out.shape[0]):
            out[pair] = totals[step][pair * 2 * SRC : (pair + 1) * 2 * SRC].astype(out.dtype)


def stack_kernel(firsts, *refs):
    refs, out = refs[:-1], refs[-1]
    for step in range(STEPS):
        for pair in range(out.shape[1] // 2):
            terms = zip(refs[step::STEPS], firsts, strict=True)
            total = sum(ref[first + pair].astype(F32) for ref, first in terms)
            out[step, 2 * pair] = total[:SRC].astype(BF16)
            out[step, 2 * pair + 1] = total[SRC:].astype(BF16)


def lagged_call(distances, plan, sources, receivers, table, dtype, carry=None, after=(), zeros=None):
    _, windows, rows, width = receivers.shape
    carry = carry or {}
    carried = sorted(carry)
    count = len({step for _, present in plan for step in present})
    operands = [*sources, receivers, table, *(carry[step] for step in carried)]
    shapes = [jax.ShapeDtypeStruct((len(distances) * rows // 2, 2 * SRC, L), dtype)] * count
    if zeros is not None:
        shapes.append(jax.ShapeDtypeStruct(zeros, BF16))
    return pl.pallas_call(
        functools.partial(lagged_kernel, distances, plan, carried, zeros is not None),
        out_shape=shapes,
        in_specs=[vmem()] * len(operands) + [pl.BlockSpec(memory_space=pl.ANY)] * len(after),
        out_specs=[vmem()] * len(shapes),
        compiler_params=params(),
        cost_estimate=pl.CostEstimate(
            flops=len(distances) * len(sources) * rows * SRC * width * L,
            bytes_accessed=2 * width * L,
            transcendentals=0,
        ),
    )(*operands, *after)


def exchange(value, axis, *distances):
    size = lax.axis_size(axis)
    return lax.ppermute(value, axis, [(i, i ^ distances[i % len(distances)]) for i in range(size)])


def body(spectra, quality, source_block):
    windows, channels, width = spectra.shape
    groups, places = lax.axis_size("chan"), lax.axis_size("win")
    bins = width // 2
    rows = channels // places
    factor = 1.0 / math.sqrt(width * windows * places)

    hbm = pl.BlockSpec(memory_space=pltpu.HBM)
    inputs = [pltpu.with_memory_space_constraint(x, pltpu.HBM) for x in (source_block, quality, spectra)]
    candidates = pl.pallas_call(
        sources_kernel,
        out_shape=[jax.ShapeDtypeStruct((windows, SRC, width // 2), BF16)] * (2 * STEPS),
        in_specs=[hbm] * 3,
        out_specs=[vmem()] * (2 * STEPS),
        scratch_shapes=[
            pltpu.SMEM(source_block.shape, jnp.int32),
            pltpu.SMEM(quality.shape, jnp.int32),
            pltpu.VMEM(spectra.shape, BF16),
            pltpu.SemaphoreType.DMA((windows + 2,)),
        ],
        compiler_params=params(),
    )(*inputs)

    table = pl.pallas_call(
        functools.partial(table_kernel, factor),
        out_shape=jax.ShapeDtypeStruct((width, L), BF16),
        out_specs=vmem(),
        scratch_shapes=[pltpu.VMEM((bins // TABLE_ROWS, L), F32)] * 2
        + [pltpu.VMEM((TABLE_ROWS, L), F32)] * 2,
        compiler_params=params(),
    )()
    mine = [candidates[step] + exchange(candidates[STEPS + step], "chan", 1) for step in range(STEPS)]
    distances = [1 << bit for bit in range(1, (groups - 1).bit_length())]
    hops = list(zip(distances, reversed(distances), strict=True))
    for index, (even, odd) in enumerate(hops):
        if index == 1:
            mine[0], table, spectra = lax.optimization_barrier((mine[0], table, spectra))
        arrived = [exchange(part, "chan", even, odd) for part in mine]
        if index < len(hops) - 1:
            mine = [part + new for part, new in zip(mine, arrived, strict=True)]
    receivers = pl.pallas_call(
        receivers_kernel,
        out_shape=jax.ShapeDtypeStruct((places, windows, rows, width), F32),
        in_specs=[smem(), vmem()],
        out_specs=vmem(),
        compiler_params=params(),
    )(quality, spectra)

    odd = [distance for distance in reversed(range(places)) if distance & 1]
    mine[0] = mine[0] + arrived[0]
    mine[0], receivers = lax.optimization_barrier((mine[0], receivers))
    other = [exchange(mine[0], "chan", 1)]
    halves = [(False, (0,)), (True, (0,))]
    (first,) = lagged_call(odd, halves, [mine[0], other[0]], receivers, table, BF16)
    mine[1] = mine[1] + arrived[1]
    other.append(exchange(mine[1], "chan", 1))
    halves = [(False, (1,)), (True, (1,))]
    (second,) = lagged_call(odd, halves, [mine[1], other[1]], receivers, table, BF16, after=[first])

    def lagged(distances, after=()):
        plan = [(True, (0, 1)), (False, (0, 1))]
        return lagged_call(distances, plan, [*other, *mine], receivers, table, F32, after=after)

    pairs = rows // 2
    received = [([distance ^ 1 for distance in odd], [exchange(part, "win", 1) for part in (first, second)])]
    last = ()
    for bit in range(1, (places - 1).bit_length()):
        group = [distance for distance in reversed(range(0, places, 1 << bit)) if distance >> bit & 1]
        sums = list(lagged(group, last))
        for order, parts in received:
            here = [order.index(distance) * pairs for distance in group]
            for step in range(STEPS):
                new = jnp.concatenate([parts[step][at : at + pairs] for at in here])
                sums[step] = sums[step] + new.astype(F32)
        sums = [part.astype(BF16) for part in sums]
        last = sums[1:]
        received.append(([distance ^ 1 << bit for distance in group], [exchange(part, "win", 1 << bit) for part in sums]))
    own = lagged([0], last)
    terms = [*own, *(part for _, parts in received for part in parts)]

    return pl.pallas_call(
        functools.partial(stack_kernel, [0, *(order.index(0) * pairs for order, _ in received)]),
        out_shape=jax.ShapeDtypeStruct((STEPS, rows, SRC, L), BF16),
        in_specs=[vmem()] * len(terms),
        out_specs=vmem(),
        compiler_params=params(),
    )(*terms)


def solution(mesh):
    return jax.shard_map(
        body,
        mesh=mesh,
        in_specs=(P("win", "chan", None), P("chan"), P()),
        out_specs=P(None, ("chan", "win"), None, None),
        check_vma=False,
    )
```

```python
import functools
import math

import jax
import jax.numpy as jnp
from jax import lax
from jax.experimental import pallas as pl
from jax.experimental.pallas import tpu as pltpu
from jax.sharding import PartitionSpec as P

L = 512
SRC = 8
STEPS = 2
LANES = 128
TILES_PER_DOT = 4
TABLE_ROWS = 64
EPS = 1e-06
F32 = jnp.float32
BF16 = jnp.bfloat16
VMEM_LIMIT = 16 * 1024 * 1024


def smem():
    return pl.BlockSpec(memory_space=pltpu.SMEM)


def vmem():
    return pl.BlockSpec(memory_space=pltpu.VMEM)


def params():
    return pltpu.CompilerParams(vmem_limit_bytes=VMEM_LIMIT)


def column(count, read):
    rows = lax.broadcasted_iota(jnp.int32, (count, 1), 0)
    result = jnp.zeros((count, 1), F32)
    for row in range(count):
        result = jnp.where(rows == row, read(row), result)
    return result


def whitened_rows(values, quality):
    energy = jnp.sum(values * values, axis=-1, keepdims=True) / (values.shape[-1] // 2)
    return (values * (quality / jnp.sqrt(energy + EPS))).astype(BF16).astype(F32)


def sources_kernel(blocks_in, quality_in, spectra_in, *rest):
    outs, (blocks, quality, spectra, sems) = rest[:-4], rest[-4:]
    windows, channels, width = spectra.shape
    bins, part = width // 2, width // 4
    copies = [
        pltpu.make_async_copy(blocks_in, blocks, sems.at[windows]),
        pltpu.make_async_copy(quality_in, quality, sems.at[windows + 1]),
    ] + [
        pltpu.make_async_copy(spectra_in.at[window], spectra.at[window], sems.at[window])
        for window in range(windows)
    ]
    for copy in copies:
        copy.start()
    copies[0].wait()
    copies[1].wait()
    group = lax.axis_index("chan")
    even = group % 2 == 0
    per_group = channels // SRC
    chosen = []
    for step in range(STEPS):
        block = blocks[step]
        held = (block // per_group == group).astype(jnp.int32)
        base = block % per_group * SRC
        flags = column(SRC, lambda row: (quality[base + row] * held).astype(F32))
        chosen.append((pl.multiple_of(base // 16 * 16, 16), base % 16 != 0, flags))
    for copy in copies[2:]:
        copy.wait()
    for window in range(windows):
        for step, (aligned, upper, flags) in enumerate(chosen):
            rows = spectra[window, pl.ds(aligned, 16), :].astype(F32)
            values = whitened_rows(jnp.where(upper, rows[SRC:], rows[:SRC]), flags)
            low = jnp.concatenate([values[:, :part], values[:, bins : bins + part]], axis=1)
            high = jnp.concatenate([values[:, part:bins], values[:, bins + part :]], axis=1)
            outs[step][window] = jnp.where(even, low, high).astype(BF16)
            outs[STEPS + step][window] = jnp.where(even, high, low).astype(BF16)


def receivers_kernel(quality, spectra, out):
    owners, windows, rows, _ = out.shape
    flags = column(owners * rows, lambda row: quality[row].astype(F32))
    for window in range(windows):
        values = whitened_rows(spectra[window].astype(F32), flags)
        for owner in range(owners):
            out[owner, window] = values[owner * rows : (owner + 1) * rows]


def table_kernel(factor, out, turn_cos, turn_sin, base_cos, base_sin):
    bins, lags = out.shape[0] // 2, out.shape[1]

    def angles(count, stride):
        rows = lax.broadcasted_iota(jnp.int32, (count, lags), 0) * stride
        shifts = lax.broadcasted_iota(jnp.int32, (count, lags), 1) - lags // 2
        residue = (rows * shifts) & (2 * bins - 1)
        residue = jnp.where(residue >= bins, residue - 2 * bins, residue)
        return residue.astype(F32) * (2.0 * math.pi / (2 * bins))

    turns = angles(bins // TABLE_ROWS, TABLE_ROWS)
    turn_cos[...] = jnp.cos(turns) * factor
    turn_sin[...] = jnp.sin(turns) * factor
    base = angles(TABLE_ROWS, 1)
    base_cos[...] = jnp.cos(base)
    base_sin[...] = jnp.sin(base)

    @pl.loop(0, bins // TABLE_ROWS)
    def _(turn):
        far_cos, far_sin = turn_cos[pl.ds(turn, 1), :], turn_sin[pl.ds(turn, 1), :]
        near_cos, near_sin = base_cos[...], base_sin[...]
        start = pl.multiple_of(turn * TABLE_ROWS, TABLE_ROWS)
        out[pl.ds(start, TABLE_ROWS), :] = (near_cos * far_cos - near_sin * far_sin).astype(BF16)
        out[pl.ds(bins + start, TABLE_ROWS), :] = (
            -(near_sin * far_cos + near_cos * far_sin)
        ).astype(BF16)


def lagged_kernel(distances, plan, *refs):
    steps = sorted({step for _, present in plan for step in present})
    count = sum(len(present) for _, present in plan)
    sources, (receivers, table), refs = list(refs[:count]), refs[count : count + 2], refs[count + 2 :]
    outs = refs[len(refs) - len(steps) :]
    core = lax.axis_index("chan") % 2
    _, windows, rows, width = receivers.shape
    bins, part = width // 2, width // 4
    depth = TILES_PER_DOT * LANES

    def cross_tile(pair, start, at):
        real, imag = pl.ds(at, LANES), pl.ds(part + at, LANES)
        src = [
            [(ref[w, :, real].astype(F32), ref[w, :, imag].astype(F32)) for w in range(windows)]
            for ref in pair
        ]
        real = pl.ds(pl.multiple_of(start + at, LANES), LANES)
        imag = pl.ds(pl.multiple_of(bins + start + at, LANES), LANES)
        found = [[], []]
        for distance in distances:
            owner = lax.axis_index("win") ^ distance
            held = []
            for row in range(rows):
                sums = [[None, None] for _ in pair]
                for w in range(windows):
                    rec_real = receivers[owner, w, pl.ds(row, 1), real]
                    rec_imag = receivers[owner, w, pl.ds(row, 1), imag]
                    for total, one in zip(sums, src, strict=True):
                        src_real, src_imag = one[w]
                        re = src_real * rec_real + src_imag * rec_imag
                        im = src_real * rec_imag - src_imag * rec_real
                        total[0] = re if w == 0 else total[0] + re
                        total[1] = im if w == 0 else total[1] + im
                held += sums
                if len(held) == 2:
                    for p in range(2):
                        found[p].append(jnp.concatenate([total[p] for total in held], axis=0).astype(BF16))
                    held = []
        return [jnp.concatenate(found[p], axis=0) for p in range(2)]

    total = None
    for other, present in plan:
        pair, sources = sources[: len(present)], sources[len(present) :]
        start = (1 - core if other else core) * part
        for chunk in range(part // depth):
            at = chunk * depth
            tiles = [cross_tile(pair, start, at + tile * LANES) for tile in range(TILES_PER_DOT)]
            for p in range(2):
                cross = jnp.concatenate([tile[p] for tile in tiles], axis=1)
                where = pl.ds(pl.multiple_of(p * bins + start + at, depth), depth)
                product = jnp.dot(cross, table[where, :], preferred_element_type=F32)
                total = product if total is None else total + product
    for place, out in enumerate(outs):
        for pair in range(out.shape[0]):
            lines = [((2 * pair + row) * len(steps) + place) * SRC for row in range(2)]
            out[pair] = jnp.concatenate([total[line : line + SRC] for line in lines], axis=0).astype(out.dtype)


def stack_kernel(firsts, *refs):
    refs, out = list(refs[:-1]), refs[-1]
    for step in range(STEPS):
        terms = list(zip(refs, firsts[step], strict=False))
        refs = refs[len(terms) :]
        for pair in range(out.shape[1] // 2):
            total = sum(ref[first + pair].astype(F32) for ref, first in terms)
            out[step, 2 * pair] = total[:SRC].astype(BF16)
            out[step, 2 * pair + 1] = total[SRC:].astype(BF16)


def lagged_call(distances, plan, sources, receivers, table, dtype, after=()):
    _, windows, rows, width = receivers.shape
    operands = [*sources, receivers, table]
    count = len({step for _, present in plan for step in present})
    shape = jax.ShapeDtypeStruct((len(distances) * rows // 2, 2 * SRC, L), dtype)
    return pl.pallas_call(
        functools.partial(lagged_kernel, distances, plan),
        out_shape=[shape] * count,
        in_specs=[vmem()] * len(operands) + [pl.BlockSpec(memory_space=pl.ANY)] * len(after),
        out_specs=[vmem()] * count,
        compiler_params=params(),
        cost_estimate=pl.CostEstimate(
            flops=len(distances) * len(sources) * rows * SRC * width * L,
            bytes_accessed=2 * width * L,
            transcendentals=0,
        ),
    )(*operands, *after)


def exchange(value, axis, *distances):
    size = lax.axis_size(axis)
    return lax.ppermute(value, axis, [(i, i ^ distances[i % len(distances)]) for i in range(size)])


def body(spectra, quality, source_block):
    windows, channels, width = spectra.shape
    groups, places = lax.axis_size("chan"), lax.axis_size("win")
    bins = width // 2
    rows = channels // places
    factor = 1.0 / math.sqrt(width * windows * places)

    hbm = pl.BlockSpec(memory_space=pltpu.HBM)
    inputs = [pltpu.with_memory_space_constraint(x, pltpu.HBM) for x in (source_block, quality, spectra)]
    candidates = pl.pallas_call(
        sources_kernel,
        out_shape=[jax.ShapeDtypeStruct((windows, SRC, width // 2), BF16)] * (2 * STEPS),
        in_specs=[hbm] * 3,
        out_specs=[vmem()] * (2 * STEPS),
        scratch_shapes=[
            pltpu.SMEM(source_block.shape, jnp.int32),
            pltpu.SMEM(quality.shape, jnp.int32),
            pltpu.VMEM(spectra.shape, BF16),
            pltpu.SemaphoreType.DMA((windows + 2,)),
        ],
        compiler_params=params(),
    )(*inputs)

    table = pl.pallas_call(
        functools.partial(table_kernel, factor),
        out_shape=jax.ShapeDtypeStruct((width, L), BF16),
        out_specs=vmem(),
        scratch_shapes=[pltpu.VMEM((bins // TABLE_ROWS, L), F32)] * 2
        + [pltpu.VMEM((TABLE_ROWS, L), F32)] * 2,
        compiler_params=params(),
    )()
    mine = [candidates[step] + exchange(candidates[STEPS + step], "chan", 1) for step in range(STEPS)]
    distances = [1 << bit for bit in range(1, (groups - 1).bit_length())]
    hops = list(zip(distances, reversed(distances), strict=True))
    for index, (even, odd) in enumerate(hops):
        if index == 1:
            mine[0], table, spectra = lax.optimization_barrier((mine[0], table, spectra))
        arrived = [exchange(part, "chan", even, odd) for part in mine]
        if index < len(hops) - 1:
            mine = [part + new for part, new in zip(mine, arrived, strict=True)]
    receivers = pl.pallas_call(
        receivers_kernel,
        out_shape=jax.ShapeDtypeStruct((places, windows, rows, width), F32),
        in_specs=[smem(), vmem()],
        out_specs=vmem(),
        compiler_params=params(),
    )(quality, spectra)

    mine[0] = mine[0] + arrived[0]
    mine[0], receivers = lax.optimization_barrier((mine[0], receivers))

    def lagged(distances, steps, dtype, after=()):
        plan = [(False, steps), (True, steps)]
        operands = [sources[step][half] for half in range(2) for step in steps]
        return lagged_call(distances, plan, operands, receivers, table, dtype, after)

    pairs = rows // 2
    received = [[] for _ in range(STEPS)]
    odd = list(reversed(range(1, places, 2)))
    sources = [(mine[0], exchange(mine[0], "chan", 1))]
    mine[1] = mine[1] + arrived[1]
    sources.append((mine[1], exchange(mine[1], "chan", 1)))
    (part,) = last = lagged(odd, (0,), BF16)
    received[0].append(([distance ^ 1 for distance in odd], exchange(part, "win", 1)))
    (part,) = last = lagged(odd, (1,), BF16, last)
    received[1].append(([distance ^ 1 for distance in odd], exchange(part, "win", 1)))
    for bit in range(1, (places - 1).bit_length()):
        group = [distance for distance in reversed(range(0, places, 1 << bit)) if distance >> bit & 1]
        sums = list(lagged(group, (0, 1), F32))
        for step in range(STEPS):
            for order, part in received[step]:
                here = [order.index(distance) * pairs for distance in group]
                new = jnp.concatenate([part[at : at + pairs] for at in here])
                sums[step] = sums[step] + new.astype(F32)
            sums[step] = sums[step].astype(BF16)
        last = tuple(sums[1:])
        for step in range(STEPS):
            received[step].append(([distance ^ 1 << bit for distance in group], exchange(sums[step], "win", 1 << bit)))
    own = lagged([0], (0, 1), F32, last)
    terms = [
        [(own[step], 0)] + [(part, (len(order) - 1) * pairs) for order, part in received[step] if order[-1] == 0]
        for step in range(STEPS)
    ]
    operands = [part for step in terms for part, _ in step]

    return pl.pallas_call(
        functools.partial(stack_kernel, [[first for _, first in step] for step in terms]),
        out_shape=jax.ShapeDtypeStruct((STEPS, rows, SRC, L), BF16),
        in_specs=[vmem()] * len(operands),
        out_specs=vmem(),
        compiler_params=params(),
    )(*operands)


def solution(mesh):
    return jax.shard_map(
        body,
        mesh=mesh,
        in_specs=(P("win", "chan", None), P("chan"), P()),
        out_specs=P(None, ("chan", "win"), None, None),
        check_vma=False,
    )
```

```python
import functools
import math

import jax
import jax.numpy as jnp
from jax import lax
from jax.experimental import pallas as pl
from jax.experimental.pallas import tpu as pltpu
from jax.sharding import PartitionSpec as P

L = 512
SRC = 8
STEPS = 2
LANES = 128
TILES_PER_DOT = 4
TABLE_ROWS = 64
EPS = 1e-06
F32 = jnp.float32
BF16 = jnp.bfloat16
VMEM_LIMIT = 16 * 1024 * 1024


def smem():
    return pl.BlockSpec(memory_space=pltpu.SMEM)


def vmem():
    return pl.BlockSpec(memory_space=pltpu.VMEM)


def params():
    return pltpu.CompilerParams(vmem_limit_bytes=VMEM_LIMIT)


def column(count, read):
    rows = lax.broadcasted_iota(jnp.int32, (count, 1), 0)
    result = jnp.zeros((count, 1), F32)
    for row in range(count):
        result = jnp.where(rows == row, read(row), result)
    return result


def scaled_rows(values, quality):
    energy = jnp.sum(values * values, axis=-1, keepdims=True) / (values.shape[-1] // 2)
    return values * (quality / jnp.sqrt(energy + EPS))


def sources_kernel(blocks_in, quality_in, spectra_in, *rest):
    outs, (blocks, quality, spectra, sems) = rest[:-4], rest[-4:]
    windows, channels, width = spectra.shape
    bins, part = width // 2, width // 4
    copies = [
        pltpu.make_async_copy(blocks_in, blocks, sems.at[windows]),
        pltpu.make_async_copy(quality_in, quality, sems.at[windows + 1]),
    ] + [
        pltpu.make_async_copy(spectra_in.at[window], spectra.at[window], sems.at[window])
        for window in range(windows)
    ]
    for copy in copies:
        copy.start()
    copies[0].wait()
    copies[1].wait()
    group = lax.axis_index("chan")
    even = group % 2 == 0
    per_group = channels // SRC
    chosen = []
    for step in range(STEPS):
        block = blocks[step]
        held = (block // per_group == group).astype(jnp.int32)
        base = block % per_group * SRC
        flags = column(SRC, lambda row: (quality[base + row] * held).astype(F32))
        chosen.append((pl.multiple_of(base // 16 * 16, 16), base % 16 != 0, flags))
    for copy in copies[2:]:
        copy.wait()
    for window in range(windows):
        for step, (aligned, upper, flags) in enumerate(chosen):
            rows = spectra[window, pl.ds(aligned, 16), :].astype(F32)
            values = scaled_rows(jnp.where(upper, rows[SRC:], rows[:SRC]), flags)
            low = jnp.concatenate([values[:, :part], values[:, bins : bins + part]], axis=1)
            high = jnp.concatenate([values[:, part:bins], values[:, bins + part :]], axis=1)
            outs[step][window] = jnp.where(even, low, high).astype(BF16)
            outs[STEPS + step][window] = jnp.where(even, high, low).astype(BF16)


def receivers_kernel(quality, spectra, out):
    owners, windows, rows, _ = out.shape
    flags = column(owners * rows, lambda row: quality[row].astype(F32))
    for window in range(windows):
        values = scaled_rows(spectra[window].astype(F32), flags).astype(BF16).astype(F32)
        for owner in range(owners):
            out[owner, window] = values[owner * rows : (owner + 1) * rows]


def table_kernel(factor, out, turn_cos, turn_sin, base_cos, base_sin):
    bins, lags = out.shape[0] // 2, out.shape[1]

    def angles(count, stride):
        rows = lax.broadcasted_iota(jnp.int32, (count, lags), 0) * stride
        shifts = lax.broadcasted_iota(jnp.int32, (count, lags), 1) - lags // 2
        residue = (rows * shifts) & (2 * bins - 1)
        residue = jnp.where(residue >= bins, residue - 2 * bins, residue)
        return residue.astype(F32) * (2.0 * math.pi / (2 * bins))

    turns = angles(bins // TABLE_ROWS, TABLE_ROWS)
    turn_cos[...] = jnp.cos(turns) * factor
    turn_sin[...] = jnp.sin(turns) * factor
    base = angles(TABLE_ROWS, 1)
    base_cos[...] = jnp.cos(base)
    base_sin[...] = jnp.sin(base)

    @pl.loop(0, bins // TABLE_ROWS)
    def _(turn):
        far_cos, far_sin = turn_cos[pl.ds(turn, 1), :], turn_sin[pl.ds(turn, 1), :]
        near_cos, near_sin = base_cos[...], base_sin[...]
        start = pl.multiple_of(turn * TABLE_ROWS, TABLE_ROWS)
        out[pl.ds(start, TABLE_ROWS), :] = (near_cos * far_cos - near_sin * far_sin).astype(BF16)
        out[pl.ds(bins + start, TABLE_ROWS), :] = (
            -(near_sin * far_cos + near_cos * far_sin)
        ).astype(BF16)


def lagged_kernel(distances, plan, *refs):
    steps = sorted({step for _, present in plan for step in present})
    count = sum(len(present) for _, present in plan)
    sources, (receivers, table), refs = list(refs[:count]), refs[count : count + 2], refs[count + 2 :]
    outs = refs[len(refs) - len(steps) :]
    core = lax.axis_index("chan") % 2
    _, windows, rows, width = receivers.shape
    bins, part = width // 2, width // 4
    depth = TILES_PER_DOT * LANES

    def cross_tile(pair, start, at):
        real, imag = pl.ds(at, LANES), pl.ds(part + at, LANES)
        src = [
            [(ref[w, :, real].astype(F32), ref[w, :, imag].astype(F32)) for w in range(windows)]
            for ref in pair
        ]
        real = pl.ds(pl.multiple_of(start + at, LANES), LANES)
        imag = pl.ds(pl.multiple_of(bins + start + at, LANES), LANES)
        found = [[], []]
        for distance in distances:
            owner = lax.axis_index("win") ^ distance
            held = []
            for row in range(rows):
                sums = [[None, None] for _ in pair]
                for w in range(windows):
                    rec_real = receivers[owner, w, pl.ds(row, 1), real]
                    rec_imag = receivers[owner, w, pl.ds(row, 1), imag]
                    for total, one in zip(sums, src, strict=True):
                        src_real, src_imag = one[w]
                        re = src_real * rec_real + src_imag * rec_imag
                        im = src_real * rec_imag - src_imag * rec_real
                        total[0] = re if w == 0 else total[0] + re
                        total[1] = im if w == 0 else total[1] + im
                held += sums
                if len(held) == 2:
                    for p in range(2):
                        found[p].append(jnp.concatenate([total[p] for total in held], axis=0).astype(BF16))
                    held = []
        return [jnp.concatenate(found[p], axis=0) for p in range(2)]

    total = None
    for other, present in plan:
        pair, sources = sources[: len(present)], sources[len(present) :]
        start = (1 - core if other else core) * part
        for chunk in range(part // depth):
            at = chunk * depth
            tiles = [cross_tile(pair, start, at + tile * LANES) for tile in range(TILES_PER_DOT)]
            for p in range(2):
                cross = jnp.concatenate([tile[p] for tile in tiles], axis=1)
                where = pl.ds(pl.multiple_of(p * bins + start + at, depth), depth)
                product = jnp.dot(cross, table[where, :], preferred_element_type=F32)
                total = product if total is None else total + product
    for place, out in enumerate(outs):
        for pair in range(out.shape[0]):
            lines = [((2 * pair + row) * len(steps) + place) * SRC for row in range(2)]
            out[pair] = jnp.concatenate([total[line : line + SRC] for line in lines], axis=0).astype(out.dtype)


def stack_kernel(firsts, *refs):
    refs, out = list(refs[:-1]), refs[-1]
    for step in range(STEPS):
        terms = list(zip(refs, firsts[step], strict=False))
        refs = refs[len(terms) :]
        for pair in range(out.shape[1] // 2):
            total = sum(ref[first + pair].astype(F32) for ref, first in terms)
            out[step, 2 * pair] = total[:SRC].astype(BF16)
            out[step, 2 * pair + 1] = total[SRC:].astype(BF16)


def lagged_call(distances, plan, sources, receivers, table, dtype, after=()):
    _, windows, rows, width = receivers.shape
    operands = [*sources, receivers, table]
    count = len({step for _, present in plan for step in present})
    shape = jax.ShapeDtypeStruct((len(distances) * rows // 2, 2 * SRC, L), dtype)
    return pl.pallas_call(
        functools.partial(lagged_kernel, distances, plan),
        out_shape=[shape] * count,
        in_specs=[vmem()] * len(operands) + [pl.BlockSpec(memory_space=pl.ANY)] * len(after),
        out_specs=[vmem()] * count,
        compiler_params=params(),
        cost_estimate=pl.CostEstimate(
            flops=len(distances) * len(sources) * rows * SRC * width * L,
            bytes_accessed=2 * width * L,
            transcendentals=0,
        ),
    )(*operands, *after)


def exchange(value, axis, *distances):
    size = lax.axis_size(axis)
    return lax.ppermute(value, axis, [(i, i ^ distances[i % len(distances)]) for i in range(size)])


def body(spectra, quality, source_block):
    windows, channels, width = spectra.shape
    groups, places = lax.axis_size("chan"), lax.axis_size("win")
    bins = width // 2
    rows = channels // places
    factor = 1.0 / math.sqrt(width * windows * places)

    hbm = pl.BlockSpec(memory_space=pltpu.HBM)
    inputs = [pltpu.with_memory_space_constraint(x, pltpu.HBM) for x in (source_block, quality, spectra)]
    candidates = pl.pallas_call(
        sources_kernel,
        out_shape=[jax.ShapeDtypeStruct((windows, SRC, width // 2), BF16)] * (2 * STEPS),
        in_specs=[hbm] * 3,
        out_specs=[vmem()] * (2 * STEPS),
        scratch_shapes=[
            pltpu.SMEM(source_block.shape, jnp.int32),
            pltpu.SMEM(quality.shape, jnp.int32),
            pltpu.VMEM(spectra.shape, BF16),
            pltpu.SemaphoreType.DMA((windows + 2,)),
        ],
        compiler_params=params(),
    )(*inputs)

    table = pl.pallas_call(
        functools.partial(table_kernel, factor),
        out_shape=jax.ShapeDtypeStruct((width, L), BF16),
        out_specs=vmem(),
        scratch_shapes=[pltpu.VMEM((bins // TABLE_ROWS, L), F32)] * 2
        + [pltpu.VMEM((TABLE_ROWS, L), F32)] * 2,
        compiler_params=params(),
    )()
    mine = [candidates[step] + exchange(candidates[STEPS + step], "chan", 1) for step in range(STEPS)]
    distances = [1 << bit for bit in range(1, (groups - 1).bit_length())]
    hops = list(zip(distances, reversed(distances), strict=True))
    for index, (even, odd) in enumerate(hops):
        if index == 1:
            mine[0], table, spectra = lax.optimization_barrier((mine[0], table, spectra))
        arrived = [exchange(part, "chan", even, odd) for part in mine]
        if index < len(hops) - 1:
            mine = [part + new for part, new in zip(mine, arrived, strict=True)]
    receivers = pl.pallas_call(
        receivers_kernel,
        out_shape=jax.ShapeDtypeStruct((places, windows, rows, width), F32),
        in_specs=[smem(), vmem()],
        out_specs=vmem(),
        compiler_params=params(),
    )(quality, spectra)

    mine[0] = mine[0] + arrived[0]
    mine[0], receivers = lax.optimization_barrier((mine[0], receivers))

    def lagged(distances, steps, dtype, after=()):
        plan = [(False, steps), (True, steps)]
        operands = [sources[step][half] for half in range(2) for step in steps]
        return lagged_call(distances, plan, operands, receivers, table, dtype, after)

    pairs = rows // 2
    received = [[] for _ in range(STEPS)]
    odd = list(reversed(range(1, places, 2)))
    sources = [(mine[0], exchange(mine[0], "chan", 1))]
    mine[1] = mine[1] + arrived[1]
    sources.append((mine[1], exchange(mine[1], "chan", 1)))
    (part,) = last = lagged(odd, (0,), BF16)
    received[0].append(([distance ^ 1 for distance in odd], exchange(part, "win", 1)))
    (part,) = last = lagged(odd, (1,), BF16, last)
    received[1].append(([distance ^ 1 for distance in odd], exchange(part, "win", 1)))
    for bit in range(1, (places - 1).bit_length()):
        group = [distance for distance in reversed(range(0, places, 1 << bit)) if distance >> bit & 1]
        sums = list(lagged(group, (0, 1), F32))
        for step in range(STEPS):
            for order, part in received[step]:
                here = [order.index(distance) * pairs for distance in group]
                new = jnp.concatenate([part[at : at + pairs] for at in here])
                sums[step] = sums[step] + new.astype(F32)
            sums[step] = sums[step].astype(BF16)
        last = tuple(sums[1:])
        for step in range(STEPS):
            received[step].append(([distance ^ 1 << bit for distance in group], exchange(sums[step], "win", 1 << bit)))
    own = lagged([0], (0, 1), F32, last)
    terms = [
        [(own[step], 0)] + [(part, (len(order) - 1) * pairs) for order, part in received[step] if order[-1] == 0]
        for step in range(STEPS)
    ]
    operands = [part for step in terms for part, _ in step]

    return pl.pallas_call(
        functools.partial(stack_kernel, [[first for _, first in step] for step in terms]),
        out_shape=jax.ShapeDtypeStruct((STEPS, rows, SRC, L), BF16),
        in_specs=[vmem()] * len(operands),
        out_specs=vmem(),
        compiler_params=params(),
    )(*operands)


def solution(mesh):
    return jax.shard_map(
        body,
        mesh=mesh,
        in_specs=(P("win", "chan", None), P("chan"), P()),
        out_specs=P(None, ("chan", "win"), None, None),
        check_vma=False,
    )
```

```python
import functools
import math

import jax
import jax.numpy as jnp
from jax import lax
from jax.experimental import pallas as pl
from jax.experimental.pallas import tpu as pltpu
from jax.sharding import PartitionSpec as P

L = 512
SRC = 8
STEPS = 2
LANES = 128
TILES_PER_DOT = 2
TABLE_ROWS = 64
EPS = 1e-06
F32 = jnp.float32
BF16 = jnp.bfloat16
VMEM_LIMIT = 16 * 1024 * 1024


def smem():
    return pl.BlockSpec(memory_space=pltpu.SMEM)


def vmem():
    return pl.BlockSpec(memory_space=pltpu.VMEM)


def params():
    return pltpu.CompilerParams(vmem_limit_bytes=VMEM_LIMIT)


def column(count, read):
    rows = lax.broadcasted_iota(jnp.int32, (count, 1), 0)
    result = jnp.zeros((count, 1), F32)
    for row in range(count):
        result = jnp.where(rows == row, read(row), result)
    return result


def scaled_rows(values, quality):
    energy = jnp.sum(values * values, axis=-1, keepdims=True) / (values.shape[-1] // 2)
    return values * (quality / jnp.sqrt(energy + EPS))


def sources_kernel(blocks_in, quality_in, spectra_in, *rest):
    outs, (blocks, quality, spectra, sems) = rest[:-4], rest[-4:]
    windows, channels, width = spectra.shape
    bins, part = width // 2, width // 4
    copies = [
        pltpu.make_async_copy(blocks_in, blocks, sems.at[windows]),
        pltpu.make_async_copy(quality_in, quality, sems.at[windows + 1]),
    ] + [
        pltpu.make_async_copy(spectra_in.at[window], spectra.at[window], sems.at[window])
        for window in range(windows)
    ]
    for copy in copies:
        copy.start()
    copies[0].wait()
    copies[1].wait()
    group = lax.axis_index("chan")
    even = group % 2 == 0
    per_group = channels // SRC
    chosen = []
    for step in range(STEPS):
        block = blocks[step]
        held = (block // per_group == group).astype(jnp.int32)
        base = block % per_group * SRC
        flags = column(SRC, lambda row: (quality[base + row] * held).astype(F32))
        chosen.append((pl.multiple_of(base // 16 * 16, 16), base % 16 != 0, flags))
    for copy in copies[2:]:
        copy.wait()
    for window in range(windows):
        for step, (aligned, upper, flags) in enumerate(chosen):
            rows = spectra[window, pl.ds(aligned, 16), :].astype(F32)
            values = scaled_rows(jnp.where(upper, rows[SRC:], rows[:SRC]), flags)
            low = jnp.concatenate([values[:, :part], values[:, bins : bins + part]], axis=1)
            high = jnp.concatenate([values[:, part:bins], values[:, bins + part :]], axis=1)
            outs[step][window] = jnp.where(even, low, high).astype(BF16)
            outs[STEPS + step][window] = jnp.where(even, high, low).astype(BF16)


def receivers_kernel(quality, spectra, out):
    owners, windows, rows, _ = out.shape
    flags = column(owners * rows, lambda row: quality[row].astype(F32))
    for window in range(windows):
        values = scaled_rows(spectra[window].astype(F32), flags).astype(BF16).astype(F32)
        for owner in range(owners):
            out[owner, window] = values[owner * rows : (owner + 1) * rows]


def table_kernel(factor, out, turn_cos, turn_sin, base_cos, base_sin):
    bins, lags = out.shape[0] // 2, out.shape[1]

    def angles(count, stride):
        rows = lax.broadcasted_iota(jnp.int32, (count, lags), 0) * stride
        shifts = lax.broadcasted_iota(jnp.int32, (count, lags), 1) - lags // 2
        residue = (rows * shifts) & (2 * bins - 1)
        residue = jnp.where(residue >= bins, residue - 2 * bins, residue)
        return residue.astype(F32) * (2.0 * math.pi / (2 * bins))

    turns = angles(bins // TABLE_ROWS, TABLE_ROWS)
    turn_cos[...] = jnp.cos(turns) * factor
    turn_sin[...] = jnp.sin(turns) * factor
    base = angles(TABLE_ROWS, 1)
    base_cos[...] = jnp.cos(base)
    base_sin[...] = jnp.sin(base)

    @pl.loop(0, bins // TABLE_ROWS)
    def _(turn):
        far_cos, far_sin = turn_cos[pl.ds(turn, 1), :], turn_sin[pl.ds(turn, 1), :]
        near_cos, near_sin = base_cos[...], base_sin[...]
        start = pl.multiple_of(turn * TABLE_ROWS, TABLE_ROWS)
        out[pl.ds(start, TABLE_ROWS), :] = (near_cos * far_cos - near_sin * far_sin).astype(BF16)
        out[pl.ds(bins + start, TABLE_ROWS), :] = (
            -(near_sin * far_cos + near_cos * far_sin)
        ).astype(BF16)


def lagged_kernel(distances, plan, *refs):
    steps = sorted({step for _, present in plan for step in present})
    count = sum(len(present) for _, present in plan)
    sources, (receivers, table), refs = list(refs[:count]), refs[count : count + 2], refs[count + 2 :]
    outs = refs[len(refs) - len(steps) :]
    core = lax.axis_index("chan") % 2
    _, windows, rows, width = receivers.shape
    bins, part = width // 2, width // 4
    depth = TILES_PER_DOT * LANES

    def cross_tile(pair, start, at):
        real, imag = pl.ds(at, LANES), pl.ds(part + at, LANES)
        src = [
            [(ref[w, :, real].astype(F32), ref[w, :, imag].astype(F32)) for w in range(windows)]
            for ref in pair
        ]
        real = pl.ds(pl.multiple_of(start + at, LANES), LANES)
        imag = pl.ds(pl.multiple_of(bins + start + at, LANES), LANES)
        found = [[], []]
        for distance in distances:
            owner = lax.axis_index("win") ^ distance
            held = []
            for row in range(rows):
                sums = [[None, None] for _ in pair]
                for w in range(windows):
                    rec_real = receivers[owner, w, pl.ds(row, 1), real]
                    rec_imag = receivers[owner, w, pl.ds(row, 1), imag]
                    for total, one in zip(sums, src, strict=True):
                        src_real, src_imag = one[w]
                        re = src_real * rec_real + src_imag * rec_imag
                        im = src_real * rec_imag - src_imag * rec_real
                        total[0] = re if w == 0 else total[0] + re
                        total[1] = im if w == 0 else total[1] + im
                held += sums
                if len(held) == 2:
                    for p in range(2):
                        found[p].append(jnp.concatenate([total[p] for total in held], axis=0).astype(BF16))
                    held = []
        return [jnp.concatenate(found[p], axis=0) for p in range(2)]

    total = None
    for other, present in plan:
        pair, sources = sources[: len(present)], sources[len(present) :]
        start = (1 - core if other else core) * part
        for chunk in range(part // depth):
            at = chunk * depth
            tiles = [cross_tile(pair, start, at + tile * LANES) for tile in range(TILES_PER_DOT)]
            for p in range(2):
                cross = jnp.concatenate([tile[p] for tile in tiles], axis=1)
                where = pl.ds(pl.multiple_of(p * bins + start + at, depth), depth)
                product = jnp.dot(cross, table[where, :], preferred_element_type=F32)
                total = product if total is None else total + product
    for place, out in enumerate(outs):
        for pair in range(out.shape[0]):
            lines = [((2 * pair + row) * len(steps) + place) * SRC for row in range(2)]
            out[pair] = jnp.concatenate([total[line : line + SRC] for line in lines], axis=0).astype(out.dtype)


def stack_kernel(firsts, *refs):
    refs, out = list(refs[:-1]), refs[-1]
    for step in range(STEPS):
        terms = list(zip(refs, firsts[step], strict=False))
        refs = refs[len(terms) :]
        for pair in range(out.shape[1] // 2):
            total = sum(ref[first + pair].astype(F32) for ref, first in terms)
            out[step, 2 * pair] = total[:SRC].astype(BF16)
            out[step, 2 * pair + 1] = total[SRC:].astype(BF16)


def lagged_call(distances, plan, sources, receivers, table, dtype, after=()):
    _, windows, rows, width = receivers.shape
    operands = [*sources, receivers, table]
    count = len({step for _, present in plan for step in present})
    shape = jax.ShapeDtypeStruct((len(distances) * rows // 2, 2 * SRC, L), dtype)
    return pl.pallas_call(
        functools.partial(lagged_kernel, distances, plan),
        out_shape=[shape] * count,
        in_specs=[vmem()] * len(operands) + [pl.BlockSpec(memory_space=pl.ANY)] * len(after),
        out_specs=[vmem()] * count,
        compiler_params=params(),
        cost_estimate=pl.CostEstimate(
            flops=len(distances) * len(sources) * rows * SRC * width * L,
            bytes_accessed=2 * width * L,
            transcendentals=0,
        ),
    )(*operands, *after)


def exchange(value, axis, *distances):
    size = lax.axis_size(axis)
    return lax.ppermute(value, axis, [(i, i ^ distances[i % len(distances)]) for i in range(size)])


def body(spectra, quality, source_block):
    windows, channels, width = spectra.shape
    groups, places = lax.axis_size("chan"), lax.axis_size("win")
    bins = width // 2
    rows = channels // places
    factor = 1.0 / math.sqrt(width * windows * places)

    hbm = pl.BlockSpec(memory_space=pltpu.HBM)
    inputs = [pltpu.with_memory_space_constraint(x, pltpu.HBM) for x in (source_block, quality, spectra)]
    candidates = pl.pallas_call(
        sources_kernel,
        out_shape=[jax.ShapeDtypeStruct((windows, SRC, width // 2), BF16)] * (2 * STEPS),
        in_specs=[hbm] * 3,
        out_specs=[vmem()] * (2 * STEPS),
        scratch_shapes=[
            pltpu.SMEM(source_block.shape, jnp.int32),
            pltpu.SMEM(quality.shape, jnp.int32),
            pltpu.VMEM(spectra.shape, BF16),
            pltpu.SemaphoreType.DMA((windows + 2,)),
        ],
        compiler_params=params(),
    )(*inputs)

    table = pl.pallas_call(
        functools.partial(table_kernel, factor),
        out_shape=jax.ShapeDtypeStruct((width, L), BF16),
        out_specs=vmem(),
        scratch_shapes=[pltpu.VMEM((bins // TABLE_ROWS, L), F32)] * 2
        + [pltpu.VMEM((TABLE_ROWS, L), F32)] * 2,
        compiler_params=params(),
    )()
    mine = [candidates[step] + exchange(candidates[STEPS + step], "chan", 1) for step in range(STEPS)]
    distances = [1 << bit for bit in range(1, (groups - 1).bit_length())]
    hops = list(zip(distances, reversed(distances), strict=True))
    for index, (even, odd) in enumerate(hops):
        if index == 1:
            mine[0], table, spectra = lax.optimization_barrier((mine[0], table, spectra))
        arrived = [exchange(part, "chan", even, odd) for part in mine]
        if index < len(hops) - 1:
            mine = [part + new for part, new in zip(mine, arrived, strict=True)]
    receivers = pl.pallas_call(
        receivers_kernel,
        out_shape=jax.ShapeDtypeStruct((places, windows, rows, width), F32),
        in_specs=[smem(), vmem()],
        out_specs=vmem(),
        compiler_params=params(),
    )(quality, spectra)

    mine[0] = mine[0] + arrived[0]
    mine[0], receivers = lax.optimization_barrier((mine[0], receivers))

    def lagged(distances, steps, dtype, after=()):
        plan = [(False, steps), (True, steps)]
        operands = [sources[step][half] for half in range(2) for step in steps]
        return lagged_call(distances, plan, operands, receivers, table, dtype, after)

    pairs = rows // 2
    received = [[] for _ in range(STEPS)]
    odd = list(reversed(range(1, places, 2)))
    sources = [(mine[0], exchange(mine[0], "chan", 1))]
    mine[1] = mine[1] + arrived[1]
    sources.append((mine[1], exchange(mine[1], "chan", 1)))
    (part,) = last = lagged(odd, (0,), BF16)
    received[0].append(([distance ^ 1 for distance in odd], exchange(part, "win", 1)))
    (part,) = last = lagged(odd, (1,), BF16, last)
    received[1].append(([distance ^ 1 for distance in odd], exchange(part, "win", 1)))
    for bit in range(1, (places - 1).bit_length()):
        group = [distance for distance in reversed(range(0, places, 1 << bit)) if distance >> bit & 1]
        sums = list(lagged(group, (0, 1), F32))
        for step in range(STEPS):
            for order, part in received[step]:
                here = [order.index(distance) * pairs for distance in group]
                new = jnp.concatenate([part[at : at + pairs] for at in here])
                sums[step] = sums[step] + new.astype(F32)
            sums[step] = sums[step].astype(BF16)
        last = tuple(sums[1:])
        for step in range(STEPS):
            received[step].append(([distance ^ 1 << bit for distance in group], exchange(sums[step], "win", 1 << bit)))
    own = lagged([0], (0, 1), F32, last)
    terms = [
        [(own[step], 0)] + [(part, (len(order) - 1) * pairs) for order, part in received[step] if order[-1] == 0]
        for step in range(STEPS)
    ]
    operands = [part for step in terms for part, _ in step]

    return pl.pallas_call(
        functools.partial(stack_kernel, [[first for _, first in step] for step in terms]),
        out_shape=jax.ShapeDtypeStruct((STEPS, rows, SRC, L), BF16),
        in_specs=[vmem()] * len(operands),
        out_specs=vmem(),
        compiler_params=params(),
    )(*operands)


def solution(mesh):
    return jax.shard_map(
        body,
        mesh=mesh,
        in_specs=(P("win", "chan", None), P("chan"), P()),
        out_specs=P(None, ("chan", "win"), None, None),
        check_vma=False,
    )
```
